32 devices in a mesh: depth: 8 (over y, x, core), outer: 4 (over z).
Axes of the slice: x: 2, y: 2, z: 4, core: 2. Of those that a mesh axis runs over, the one named last changes fastest.
Arguments:
- density: float32 [256, 16, 1024], P(('depth', 'outer')), may hold values from -16 to 16
- materials: int32 [256, 4, 256], P(('depth', 'outer')), may hold values from 0 to 15
- colors: float32 [3, 16], replicated, may hold values from 0.1 to 1
- opacity: float32 [16], replicated, may hold values from 2e-05 to 0.003
Outputs:
- picture: float32 [3, 16384], P(None, ('depth', 'outer'))
The draws below stay inside these ranges and needn't reach their ends.
All inputs are finite; a program needn't handle non-finite values.
Results may differ from the reference program's by a relative error of at most 0.0003.
Values sent between devices are 32-bit elements; how exact they have to be, the bound alone decides.
A program may use at most 64 MiB of HBM per device.

```python
import math
import jax
import jax.numpy as jnp
import numpy as np
from jax import lax

NX = 1024
NY = 16
PZ = 8
MATS = 16
NZ = 256


def set_ends(values, own_key, smallest, largest):
    longest = values.shape.index(max(values.shape))
    spots = []
    for shift in (0, 1):
        where = [jax.random.randint(jax.random.fold_in(own_key, axis), (), 0, length) for axis, length in enumerate(values.shape)]
        where[longest] = (where[longest] + shift) % values.shape[longest]
        spots.append(tuple(where))
    return values.at[spots[0]].set(smallest).at[spots[1]].set(largest)


def block_levels(own_key, shape, pieces, least, high):
    level, own = 1.0, jax.random.fold_in(own_key, 6)
    for axis_at, blocks in pieces:
        steps = jnp.exp(jax.random.uniform(jax.random.fold_in(own, axis_at), (blocks,), jnp.float32, least / len(pieces), high / len(pieces)))
        level = level * jnp.repeat(steps, shape[axis_at] // blocks).reshape([-1 if axis == axis_at else 1 for axis in range(len(shape))])
    return level


def cumulative_ranks(amount, slope):
    weights = [(1 << 20) // math.isqrt(standing ** slope) + 1 for standing in range(1, amount + 1)]
    scale = 1 + sum(weights) // (1 << 30)
    return np.cumsum(np.array([max(1, weight // scale) for weight in weights]))


def skewed_ids(stream_key, shape, amount, lean):
    listing = cumulative_ranks(amount, lean)
    pick = jax.random.randint(jax.random.fold_in(stream_key, 1), shape, 0, int(listing[amount - 1]))
    rank = jnp.searchsorted(jnp.asarray(listing, jnp.int32), pick, side="right")
    return jax.random.permutation(jax.random.fold_in(stream_key, 2), amount)[rank].astype(jnp.int32)


def centred(stream_key, shape, width, limit, pieces=(), kind=jnp.bfloat16):
    array = width * jax.random.normal(stream_key, shape, jnp.float32)
    if pieces:
        array = array * block_levels(stream_key, shape, pieces, -0.22, 0.18)
    return jnp.clip(array, -limit, limit).astype(kind)


def setup_inputs(seed: int = 0) -> dict:
    streams_of = jax.random.split(jax.random.key(seed), 5)
    return {
        "density": centred(streams_of[0], (NZ, NY, NX), 4.0, 16.0, ((0, 32),), jnp.float32),
        "materials": set_ends(skewed_ids(streams_of[1], (NZ, NY // 4, NX // 4), MATS, 2), jax.random.fold_in(streams_of[1], 3), 0, MATS - 1).astype(jnp.int32),
        "colors": jnp.clip(jax.random.uniform(streams_of[2], (3, MATS), jnp.float32, 0.1, 1.0), 0.1, 1.0),
        "opacity": jnp.clip(jnp.exp(jax.random.uniform(streams_of[3], (MATS,), jnp.float32, math.log(1.9999999494757503e-05), math.log(0.003))), 1.9999999494757503e-05, 0.003),
    }


LIGHT_DIR = (0.64, 0.48, 0.6)

def smooth_pass(volume, inside):
    padded = jnp.pad(volume, 1)
    beside = padded[2:, 1:-1, 1:-1] + padded[:-2, 1:-1, 1:-1]
    beside = beside + padded[1:-1, 2:, 1:-1] + padded[1:-1, :-2, 1:-1]
    beside = beside + padded[1:-1, 1:-1, 2:] + padded[1:-1, 1:-1, :-2]
    return jnp.where(inside, 0.25 * volume + 0.125 * beside, 0.0)

def derive(volume, axis):
    length = volume.shape[axis]
    widths = [(0, 0), (0, 0), (0, 0)]
    widths[axis] = (2, 2)
    padded = jnp.pad(volume, widths)

    def part(offset):
        return lax.slice_in_dim(padded, offset, offset + length, 1, axis)
    return (part(3) - part(1) + 2.0 * (part(4) - part(0))) / 10.0

def render_slab(extended, labels, first_plane, total_planes, colors, opacity):
    planes = extended.shape[0]
    depth_own = planes - 8
    global_plane = first_plane - 4 + jnp.arange(planes, dtype=jnp.int32)
    inside = ((global_plane >= 0) & (global_plane < total_planes))[:, None, None]
    volume = jnp.where(inside, extended.astype(jnp.float32), 0.0)
    volume = smooth_pass(volume, inside)
    volume = smooth_pass(volume, inside)
    smoothed = volume[2:depth_own + 6]
    grad_depth = (smoothed[3:depth_own + 3] - smoothed[1:depth_own + 1] + 2.0 * (smoothed[4:depth_own + 4] - smoothed[0:depth_own])) / 10.0
    center = smoothed[2:depth_own + 2]
    grad_rows = derive(center, 1)
    grad_cols = derive(center, 2)
    facing = LIGHT_DIR[0] * grad_depth + LIGHT_DIR[1] * grad_rows + LIGHT_DIR[2] * grad_cols
    length_sq = grad_depth * grad_depth + grad_rows * grad_rows + grad_cols * grad_cols + 1.0
    shading = 0.1 + 0.9 * jnp.abs(facing) / jnp.sqrt(length_sq)
    fine_labels = jnp.repeat(jnp.repeat(labels, 4, axis=1), 4, axis=2)
    alphas = jnp.zeros(center.shape, jnp.float32)
    tinted = jnp.zeros((3,) + center.shape, jnp.float32)
    for label_id in range(colors.shape[1]):
        chosen = fine_labels == label_id
        alphas = jnp.where(chosen, opacity[label_id], alphas)
        tinted = jnp.where(chosen[None], colors[:, label_id][:, None, None, None], tinted)
    alphas = alphas * jax.nn.sigmoid(2.0 * center)
    emitted = tinted * (alphas * shading)[None]
    radiance = jnp.zeros((3,) + center.shape[1:], jnp.float32)
    transmit = jnp.ones(center.shape[1:], jnp.float32)
    for plane_at in range(depth_own):
        radiance = radiance + transmit * emitted[:, plane_at]
        transmit = transmit * (1.0 - alphas[plane_at])
    return (radiance, transmit)

def reference(density, materials, colors, opacity):
    padded = jnp.pad(density, ((4, 4), (0, 0), (0, 0)))
    blocks = NZ // PZ

    def advance(carry, block_at):
        radiance, transmit = carry
        start = (block_at * PZ).astype(jnp.int32)
        extended = lax.dynamic_slice_in_dim(padded, start, PZ + 8, 0)
        labels = lax.dynamic_slice_in_dim(materials, start, PZ, 0)
        slab_light, slab_pass = render_slab(extended, labels, start, NZ, colors, opacity)
        return ((radiance + transmit * slab_light, transmit * slab_pass), None)
    init = (jnp.zeros((3, NY, NX), jnp.float32), jnp.ones((NY, NX), jnp.float32))
    (radiance, transmit), unused = lax.scan(advance, init, jnp.arange(blocks, dtype=jnp.int32))
    return 1.0 - jnp.exp(-4.0 * radiance.reshape(3, NY * NX))
```

```python
import functools

import jax
import jax.numpy as jnp
from jax import lax
from jax.experimental import pallas as pl
from jax.experimental.pallas import tpu as pltpu
from jax.sharding import PartitionSpec as P

LIGHT_DIR = (0.64, 0.48, 0.6)
MESH = pl.DeviceIdType.MESH
LANES = 128
HALO = 4
BLOCK = 4
CHANNELS = 4


def shifted(values, amount, axis, at_low, at_high):
    length = values.shape[axis]
    moved = pltpu.roll(values, (-amount) % length, axis)
    index = lax.broadcasted_iota(jnp.int32, values.shape, axis)
    if amount < 0 and at_low:
        moved = jnp.where(index < -amount, 0.0, moved)
    if amount > 0 and at_high:
        moved = jnp.where(index >= length - amount, 0.0, moved)
    return moved


def render_kernel(
    plan, density, materials, colors, opacity, out, ext, first, second, labels, spread, coarse, table,
    pieces, inbox, own_sem, label_sem, halo_send, halo_recv, piece_send, piece_recv,
):
    count, group, direct = plan["count"], plan["group"], plan["direct"]
    depth_own, rows, cols = density.shape
    depth_at, outer_at = lax.axis_index("depth"), lax.axis_index("outer")
    me = depth_at * group + outer_at
    planes = depth_own + 2 * HALO

    def device(position):
        return (lax.div(position, group), lax.rem(position, group))

    own_copy = pltpu.make_async_copy(density, ext.at[pl.ds(HALO, depth_own)], own_sem)
    own_copy.start()
    label_copy = pltpu.make_async_copy(materials, labels, label_sem)
    label_copy.start()

    barrier = pltpu.get_barrier_semaphore()
    if direct:
        @pl.loop(1, count)
        def _(step):
            pl.semaphore_signal(barrier, inc=1, device_id=device(lax.rem(me + step, count)), device_id_type=MESH)
        pl.semaphore_wait(barrier, count - 1)
    else:
        for away, there in ((-1, me > 0), (1, me < count - 1)):
            @pl.when(there)
            def _(away=away):
                pl.semaphore_signal(barrier, inc=1, device_id=device(me + away), device_id_type=MESH)
        for there in (me > 0, me < count - 1):
            @pl.when(there)
            def _():
                pl.semaphore_wait(barrier, 1)

    width = plan["width"]
    chunks = cols // width
    ends = [min((at + 1) * width + LANES, cols) for at in range(chunks)]
    begins = [0] + ends[:-1]

    def halo_copy(side, at):
        lanes = pl.ds(begins[at], ends[at] - begins[at])
        if side == 0:
            source, target, to = depth_own - HALO, 0, lax.rem(me + 1, count)
        else:
            source, target, to = 0, depth_own + HALO, lax.rem(me + count - 1, count)
        return pltpu.make_async_remote_copy(
            src_ref=density.at[pl.ds(source, HALO), :, lanes],
            dst_ref=ext.at[pl.ds(target, HALO), :, lanes],
            send_sem=halo_send.at[side, at],
            recv_sem=halo_recv.at[side, at],
            device_id=device(to),
            device_id_type=MESH,
        )

    sends = ((0, me < count - 1), (1, me > 0))
    receives = ((0, me > 0), (1, me < count - 1))
    for at in range(chunks):
        if begins[at] < ends[at]:
            for side, there in sends:
                @pl.when(there)
                def _(side=side, at=at):
                    halo_copy(side, at).start()

    @pl.when(me == 0)
    def _():
        ext[pl.ds(0, HALO)] = jnp.zeros((HALO, rows, cols), jnp.float32)

    @pl.when(me == count - 1)
    def _():
        ext[pl.ds(depth_own + HALO, HALO)] = jnp.zeros((HALO, rows, cols), jnp.float32)

    fine = BLOCK * LANES
    row_at = lax.rem(lax.broadcasted_iota(jnp.int32, (2 * LANES, fine), 0), LANES)
    col_at = lax.div(lax.broadcasted_iota(jnp.int32, (2 * LANES, fine), 1), BLOCK)
    spread[...] = jnp.where(row_at == col_at, 1.0, 0.0).astype(jnp.bfloat16)
    label_copy.wait()
    tiles = cols // fine

    @pl.loop(0, depth_own)
    def _(plane):
        index = labels[plane]
        index = jnp.concatenate(
            [jnp.broadcast_to(index[row : row + 1], (BLOCK, index.shape[1])) for row in range(rows // BLOCK)], 0
        )
        found = [jnp.zeros(index.shape, jnp.float32) for channel in range(CHANNELS)]
        for material in range(colors.shape[1]):
            chosen = index == material
            for channel in range(CHANNELS - 1):
                found[channel] = jnp.where(chosen, colors[channel, material], found[channel])
            found[-1] = jnp.where(chosen, 0.5 * opacity[material], found[-1])
        for channel in range(CHANNELS):
            high = found[channel].astype(jnp.bfloat16)
            low = (found[channel] - high.astype(jnp.float32)).astype(jnp.bfloat16)
            start = pl.multiple_of((plane * CHANNELS + channel) * rows, rows)
            for tile in range(tiles):
                lanes = slice(tile * LANES, (tile + 1) * LANES)
                coarse[tile, pl.ds(start, rows), :LANES] = high[:, lanes]
                coarse[tile, pl.ds(start, rows), LANES:] = low[:, lanes]

    for tile in range(tiles):
        table[:, tile * fine : (tile + 1) * fine] = jnp.dot(
            coarse[tile], spread[...], preferred_element_type=jnp.float32
        )

    def smooth(source, target, start, stop, low, high):
        lanes = pl.ds(low, high - low)

        @pl.loop(start, stop)
        def _(plane):
            where = me * depth_own - HALO + plane
            inside = jnp.where((where >= 0) & (where < count * depth_own), 1.0, 0.0)
            center = source[plane, :, lanes]
            beside = source[plane - 1, :, lanes] + source[plane + 1, :, lanes]
            beside += shifted(center, -1, 0, True, True) + shifted(center, 1, 0, True, True)
            beside += shifted(center, -1, 1, low == 0, high == cols) + shifted(center, 1, 1, low == 0, high == cols)
            target[plane, :, lanes] = (0.25 * inside) * center + (0.125 * inside) * beside

    own_copy.wait()
    smooth(ext, first, HALO + 1, planes - HALO - 1, 0, cols)
    smooth(first, second, HALO + 2, planes - HALO - 2, 0, cols)

    def differences(minus, plus, minus_two, plus_two):
        return ((plus - minus) + 2.0 * (plus_two - minus_two)) * 0.1

    block = min(width, 2 * LANES)
    for at in range(chunks):
        if begins[at] < ends[at]:
            for side, there in receives:
                @pl.when(there)
                def _(side=side, at=at):
                    halo_copy(side, at).wait_recv()
        low, high = max(at * width - LANES, 0), ends[at]
        smooth(ext, first, 1, HALO + 1, low, high)
        smooth(ext, first, planes - HALO - 1, planes - 1, low, high)
        smooth(first, second, 2, HALO + 2, low, high)
        smooth(first, second, planes - HALO - 2, planes - 2, low, high)
        for base in range(at * width, (at + 1) * width, block):
            left, right = max(base - LANES, 0), min(base + block + LANES, cols)

            def shade(plane, carry, base=base, left=left, right=right):
                light, transmit = carry[:3], carry[3]
                own = pl.ds(base, block)
                slot = plane + HALO
                center = second[slot, :, own]
                along = functools.partial(shifted, center, axis=0, at_low=True, at_high=True)
                wide = second[slot, :, pl.ds(left, right - left)]

                def across(amount):
                    moved = shifted(wide, amount, 1, left == 0, right == cols)
                    return moved[:, base - left : base - left + block]

                grad_depth = differences(*(second[slot + step, :, own] for step in (-1, 1, -2, 2)))
                grad_rows = differences(*(along(step) for step in (-1, 1, -2, 2)))
                grad_cols = differences(*(across(step) for step in (-1, 1, -2, 2)))
                facing = LIGHT_DIR[0] * grad_depth + LIGHT_DIR[1] * grad_rows + LIGHT_DIR[2] * grad_cols
                length_sq = grad_depth * grad_depth + grad_rows * grad_rows + grad_cols * grad_cols + 1.0
                shading = 0.1 + 0.9 * jnp.abs(facing) * lax.rsqrt(length_sq)

                def looked_up(channel):
                    start = pl.multiple_of((plane * CHANNELS + channel) * rows, rows)
                    return table[pl.ds(start, rows), own]

                stopped = transmit * (looked_up(3) * (1.0 + jnp.tanh(center)))
                shaded = stopped * shading
                light = tuple(light[channel] + looked_up(channel) * shaded for channel in range(3))
                return light + (transmit - stopped,)

            empty = jnp.zeros((rows, block), jnp.float32)
            layers = lax.fori_loop(0, depth_own, shade, (empty, empty, empty, empty + 1.0))
            for channel in range(CHANNELS):
                if not direct:
                    out[channel, :, pl.ds(base, block)] = layers[channel]
                    continue
                strips = width // LANES
                for strip in range(block // LANES):
                    slot = (base - at * width) // LANES + strip
                    start = at * CHANNELS * strips + channel * strips + slot
                    pieces[pl.ds(start, rows, stride=chunks * CHANNELS * strips), :] = layers[channel][
                        :, strip * LANES : (strip + 1) * LANES
                    ]
        if direct:
            size = CHANNELS * width // LANES

            @pl.loop(0, rows)
            def _(row, at=at):
                to = row * chunks + at
                here = pl.ds(pl.multiple_of(to * size, size), size)
                there = pl.ds(pl.multiple_of(me * size, size), size)

                @pl.when(to != me)
                def _():
                    pltpu.make_async_remote_copy(
                        src_ref=pieces.at[here],
                        dst_ref=inbox.at[there],
                        send_sem=piece_send,
                        recv_sem=piece_recv,
                        device_id=device(to),
                        device_id_type=MESH,
                    ).start()

                @pl.when(to == me)
                def _():
                    inbox[there, :] = pieces[here, :]

    if direct:
        size = CHANNELS * width // LANES
        strips = width // LANES
        others = pl.ds(0, (count - 1) * size)
        everything = pltpu.make_async_remote_copy(
            src_ref=pieces.at[others],
            dst_ref=inbox.at[others],
            send_sem=piece_send,
            recv_sem=piece_recv,
            device_id=device(lax.rem(me + 1, count)),
            device_id_type=MESH,
        )
        everything.wait_recv()
        total = [jnp.zeros((strips, LANES), jnp.float32) for channel in range(3)]
        left_over = jnp.ones((strips, LANES), jnp.float32)
        for source in range(count):
            base = source * size
            for channel in range(3):
                total[channel] += left_over * inbox[base + channel * strips : base + (channel + 1) * strips, :]
            left_over = left_over * inbox[base + 3 * strips : base + 4 * strips, :]
        for channel in range(3):
            toned = 1.0 - jnp.exp(-4.0 * total[channel])
            for strip in range(strips):
                out[channel : channel + 1, strip * LANES : (strip + 1) * LANES] = toned[strip : strip + 1]
        everything.wait_send()
    for at in range(chunks):
        if begins[at] < ends[at]:
            for side, there in sends:
                @pl.when(there)
                def _(side=side, at=at):
                    halo_copy(side, at).wait_send()


def over_blend(front_part, back_part):
    transmit = front_part[3:4]
    return jnp.concatenate([front_part[:3] + transmit * back_part[:3], transmit * back_part[3:4]], 0)


def blend_group(received):
    blended = received
    while blended.shape[2] > 1:
        channels, items, sources, owned = blended.shape
        paired = blended.reshape(channels, items, sources // 2, 2, owned)
        blended = over_blend(paired[:, :, :, 0, :], paired[:, :, :, 1, :])
    return blended[:, :, 0, :]


def on_device(density, materials, colors, opacity):
    depth_count, group = lax.axis_size("depth"), lax.axis_size("outer")
    count = depth_count * group
    depth_own, rows, cols = density.shape
    owned = rows * cols // count
    direct = owned % (2 * LANES) == 0 and cols % owned == 0
    width = owned if direct else cols
    size = CHANNELS * width // LANES if direct else 8
    planes = depth_own + 2 * HALO
    out_shape = (3, owned) if direct else (CHANNELS, rows, cols)
    chunks = cols // width
    volume = pltpu.VMEM((planes, rows, cols), jnp.float32)
    tiles = cols // (BLOCK * LANES)
    layers = pl.pallas_call(
        functools.partial(render_kernel, dict(count=count, group=group, direct=direct, width=width)),
        out_shape=jax.ShapeDtypeStruct(out_shape, jnp.float32),
        in_specs=[
            pl.BlockSpec(memory_space=pl.ANY),
            pl.BlockSpec(memory_space=pl.ANY),
            pl.BlockSpec(memory_space=pltpu.SMEM),
            pl.BlockSpec(memory_space=pltpu.SMEM),
        ],
        out_specs=pl.BlockSpec(memory_space=pltpu.VMEM),
        scratch_shapes=[
            volume,
            volume,
            volume,
            pltpu.VMEM(materials.shape, jnp.int32),
            pltpu.VMEM((2 * LANES, BLOCK * LANES), jnp.bfloat16),
            pltpu.VMEM((tiles, CHANNELS * depth_own * rows, 2 * LANES), jnp.bfloat16),
            pltpu.VMEM((CHANNELS * depth_own * rows, cols), jnp.float32),
            pltpu.VMEM((count * size, LANES), jnp.float32),
            pltpu.VMEM((count * size, LANES), jnp.float32),
            pltpu.SemaphoreType.DMA,
            pltpu.SemaphoreType.DMA,
            pltpu.SemaphoreType.DMA((2, chunks)),
            pltpu.SemaphoreType.DMA((2, chunks)),
            pltpu.SemaphoreType.DMA,
            pltpu.SemaphoreType.DMA,
        ],
        compiler_params=pltpu.CompilerParams(
            collective_id=0, has_side_effects=True, vmem_limit_bytes=24 * 1024 * 1024
        ),
    )(density, materials, colors, opacity)
    if direct:
        return layers
    layers = layers.reshape(CHANNELS, depth_count, group, owned)
    merged = blend_group(lax.all_to_all(layers, "outer", split_axis=2, concat_axis=2, tiled=True))
    stacked = merged.reshape(CHANNELS, 1, depth_count, owned)
    layers = blend_group(lax.all_to_all(stacked, "depth", split_axis=2, concat_axis=2, tiled=True))
    return 1.0 - jnp.exp(-4.0 * layers.reshape(CHANNELS, owned)[:3])


def solution(mesh):
    placed = (P(("depth", "outer"), None, None), P(("depth", "outer"), None, None), P(), P())
    return jax.shard_map(
        on_device,
        mesh=mesh,
        in_specs=placed,
        out_specs=P(None, ("depth", "outer")),
        check_vma=False,
    )
```

```python
import functools

import jax
import jax.numpy as jnp
from jax import lax
from jax.experimental import pallas as pl
from jax.experimental.pallas import tpu as pltpu
from jax.sharding import PartitionSpec as P

LIGHT_DIR = (0.64, 0.48, 0.6)
MESH = pl.DeviceIdType.MESH
LANES = 128
HALO = 4
BLOCK = 4
CHANNELS = 4


def shifted(values, amount, axis, at_low, at_high):
    length = values.shape[axis]
    moved = pltpu.roll(values, (-amount) % length, axis)
    index = lax.broadcasted_iota(jnp.int32, values.shape, axis)
    if amount < 0 and at_low:
        moved = jnp.where(index < -amount, 0.0, moved)
    if amount > 0 and at_high:
        moved = jnp.where(index >= length - amount, 0.0, moved)
    return moved


def render_kernel(
    plan, density, materials, colors, opacity, out, ext, first, second, labels, spread, coarse, table,
    pieces, inbox, own_sem, label_sem, halo_send, halo_recv, piece_send, piece_recv,
):
    count, group, direct = plan["count"], plan["group"], plan["direct"]
    depth_own, rows, cols = density.shape
    depth_at, outer_at = lax.axis_index("depth"), lax.axis_index("outer")
    me = depth_at * group + outer_at
    planes = depth_own + 2 * HALO

    def device(position):
        return (lax.div(position, group), lax.rem(position, group))

    own_copy = pltpu.make_async_copy(density, ext.at[pl.ds(HALO, depth_own)], own_sem)
    own_copy.start()
    label_copy = pltpu.make_async_copy(materials, labels, label_sem)
    label_copy.start()

    barrier = pltpu.get_barrier_semaphore()
    if direct:
        @pl.loop(1, count)
        def _(step):
            pl.semaphore_signal(barrier, inc=1, device_id=device(lax.rem(me + step, count)), device_id_type=MESH)
        pl.semaphore_wait(barrier, count - 1)
    else:
        for away, there in ((-1, me > 0), (1, me < count - 1)):
            @pl.when(there)
            def _(away=away):
                pl.semaphore_signal(barrier, inc=1, device_id=device(me + away), device_id_type=MESH)
        for there in (me > 0, me < count - 1):
            @pl.when(there)
            def _():
                pl.semaphore_wait(barrier, 1)

    width = plan["width"]
    chunks = cols // width
    ends = [min((at + 1) * width + LANES, cols) for at in range(chunks)]
    begins = [0] + ends[:-1]

    def halo_copy(side, at):
        lanes = pl.ds(begins[at], ends[at] - begins[at])
        if side == 0:
            source, target, to = depth_own - HALO, 0, lax.rem(me + 1, count)
        else:
            source, target, to = 0, depth_own + HALO, lax.rem(me + count - 1, count)
        return pltpu.make_async_remote_copy(
            src_ref=density.at[pl.ds(source, HALO), :, lanes],
            dst_ref=ext.at[pl.ds(target, HALO), :, lanes],
            send_sem=halo_send.at[side, at],
            recv_sem=halo_recv.at[side, at],
            device_id=device(to),
            device_id_type=MESH,
        )

    sends = ((0, me < count - 1), (1, me > 0))
    receives = ((0, me > 0), (1, me < count - 1))
    for at in range(chunks):
        if begins[at] < ends[at]:
            for side, there in sends:
                @pl.when(there)
                def _(side=side, at=at):
                    halo_copy(side, at).start()

    @pl.when(me == 0)
    def _():
        ext[pl.ds(0, HALO)] = jnp.zeros((HALO, rows, cols), jnp.float32)

    @pl.when(me == count - 1)
    def _():
        ext[pl.ds(depth_own + HALO, HALO)] = jnp.zeros((HALO, rows, cols), jnp.float32)

    fine = BLOCK * LANES
    row_at = lax.rem(lax.broadcasted_iota(jnp.int32, (2 * LANES, fine), 0), LANES)
    col_at = lax.div(lax.broadcasted_iota(jnp.int32, (2 * LANES, fine), 1), BLOCK)
    spread[...] = jnp.where(row_at == col_at, 1.0, 0.0).astype(jnp.bfloat16)
    label_copy.wait()
    tiles = cols // fine

    @pl.loop(0, depth_own, unroll=2)
    def _(plane):
        index = labels[plane]
        index = jnp.concatenate(
            [jnp.broadcast_to(index[row : row + 1], (BLOCK, index.shape[1])) for row in range(rows // BLOCK)], 0
        )
        found = [jnp.zeros(index.shape, jnp.float32) for channel in range(CHANNELS)]
        for material in range(colors.shape[1]):
            chosen = index == material
            for channel in range(CHANNELS - 1):
                found[channel] = jnp.where(chosen, colors[channel, material], found[channel])
            found[-1] = jnp.where(chosen, 0.5 * opacity[material], found[-1])
        for channel in range(CHANNELS):
            high = found[channel].astype(jnp.bfloat16)
            low = (found[channel] - high.astype(jnp.float32)).astype(jnp.bfloat16)
            start = pl.multiple_of((plane * CHANNELS + channel) * rows, rows)
            for tile in range(tiles):
                lanes = slice(tile * LANES, (tile + 1) * LANES)
                coarse[tile, pl.ds(start, rows), :LANES] = high[:, lanes]
                coarse[tile, pl.ds(start, rows), LANES:] = low[:, lanes]

    for tile in range(tiles):
        table[:, tile * fine : (tile + 1) * fine] = jnp.dot(
            coarse[tile], spread[...], preferred_element_type=jnp.float32
        )

    def smooth(source, target, start, stop, low, high):
        lanes = pl.ds(low, high - low)

        @pl.loop(start, stop, unroll=True)
        def _(plane):
            where = me * depth_own - HALO + plane
            inside = jnp.where((where >= 0) & (where < count * depth_own), 1.0, 0.0)
            center = source[plane, :, lanes]
            beside = source[plane - 1, :, lanes] + source[plane + 1, :, lanes]
            beside += shifted(center, -1, 0, True, True) + shifted(center, 1, 0, True, True)
            beside += shifted(center, -1, 1, low == 0, high == cols) + shifted(center, 1, 1, low == 0, high == cols)
            target[plane, :, lanes] = (0.25 * inside) * center + (0.125 * inside) * beside

    own_copy.wait()
    smooth(ext, first, HALO + 1, planes - HALO - 1, 0, cols)
    smooth(first, second, HALO + 2, planes - HALO - 2, 0, cols)

    def differences(minus, plus, minus_two, plus_two):
        return ((plus - minus) + 2.0 * (plus_two - minus_two)) * 0.1

    block = min(width, 2 * LANES)
    for at in range(chunks):
        if begins[at] < ends[at]:
            for side, there in receives:
                @pl.when(there)
                def _(side=side, at=at):
                    halo_copy(side, at).wait_recv()
        low, high = max(at * width - LANES, 0), ends[at]
        smooth(ext, first, 1, HALO + 1, low, high)
        smooth(ext, first, planes - HALO - 1, planes - 1, low, high)
        smooth(first, second, 2, HALO + 2, low, high)
        smooth(first, second, planes - HALO - 2, planes - 2, low, high)
        for base in range(at * width, (at + 1) * width, block):
            left, right = max(base - LANES, 0), min(base + block + LANES, cols)

            def shade(plane, carry, base=base, left=left, right=right):
                light, transmit = carry[:3], carry[3]
                own = pl.ds(base, block)
                slot = plane + HALO
                center = second[slot, :, own]
                along = functools.partial(shifted, center, axis=0, at_low=True, at_high=True)
                wide = second[slot, :, pl.ds(left, right - left)]

                def across(amount):
                    moved = shifted(wide, amount, 1, left == 0, right == cols)
                    return moved[:, base - left : base - left + block]

                grad_depth = differences(*(second[slot + step, :, own] for step in (-1, 1, -2, 2)))
                grad_rows = differences(*(along(step) for step in (-1, 1, -2, 2)))
                grad_cols = differences(*(across(step) for step in (-1, 1, -2, 2)))
                facing = LIGHT_DIR[0] * grad_depth + LIGHT_DIR[1] * grad_rows + LIGHT_DIR[2] * grad_cols
                length_sq = grad_depth * grad_depth + grad_rows * grad_rows + grad_cols * grad_cols + 1.0
                shading = 0.1 + 0.9 * jnp.abs(facing) * lax.rsqrt(length_sq)

                def looked_up(channel):
                    start = pl.multiple_of((plane * CHANNELS + channel) * rows, rows)
                    return table[pl.ds(start, rows), own]

                stopped = transmit * (looked_up(3) * (1.0 + jnp.tanh(center)))
                shaded = stopped * shading
                light = tuple(light[channel] + looked_up(channel) * shaded for channel in range(3))
                return light + (transmit - stopped,)

            empty = jnp.zeros((rows, block), jnp.float32)
            layers = lax.fori_loop(0, depth_own, shade, (empty, empty, empty, empty + 1.0), unroll=True)
            for channel in range(CHANNELS):
                if not direct:
                    out[channel, :, pl.ds(base, block)] = layers[channel]
                    continue
                strips = width // LANES
                for strip in range(block // LANES):
                    slot = (base - at * width) // LANES + strip
                    start = at * CHANNELS * strips + channel * strips + slot
                    pieces[pl.ds(start, rows, stride=chunks * CHANNELS * strips), :] = layers[channel][
                        :, strip * LANES : (strip + 1) * LANES
                    ]
        if direct:
            size = CHANNELS * width // LANES

            @pl.loop(0, rows)
            def _(row, at=at):
                to = row * chunks + at
                here = pl.ds(pl.multiple_of(to * size, size), size)
                there = pl.ds(pl.multiple_of(me * size, size), size)

                @pl.when(to != me)
                def _():
                    pltpu.make_async_remote_copy(
                        src_ref=pieces.at[here],
                        dst_ref=inbox.at[there],
                        send_sem=piece_send,
                        recv_sem=piece_recv,
                        device_id=device(to),
                        device_id_type=MESH,
                    ).start()

                @pl.when(to == me)
                def _():
                    inbox[there, :] = pieces[here, :]

    if direct:
        size = CHANNELS * width // LANES
        strips = width // LANES
        others = pl.ds(0, (count - 1) * size)
        everything = pltpu.make_async_remote_copy(
            src_ref=pieces.at[others],
            dst_ref=inbox.at[others],
            send_sem=piece_send,
            recv_sem=piece_recv,
            device_id=device(lax.rem(me + 1, count)),
            device_id_type=MESH,
        )
        everything.wait_recv()
        total = [jnp.zeros((strips, LANES), jnp.float32) for channel in range(3)]
        left_over = jnp.ones((strips, LANES), jnp.float32)
        for source in range(count):
            base = source * size
            for channel in range(3):
                total[channel] += left_over * inbox[base + channel * strips : base + (channel + 1) * strips, :]
            left_over = left_over * inbox[base + 3 * strips : base + 4 * strips, :]
        for channel in range(3):
            toned = 1.0 - jnp.exp(-4.0 * total[channel])
            for strip in range(strips):
                out[channel : channel + 1, strip * LANES : (strip + 1) * LANES] = toned[strip : strip + 1]
        everything.wait_send()
    for at in range(chunks):
        if begins[at] < ends[at]:
            for side, there in sends:
                @pl.when(there)
                def _(side=side, at=at):
                    halo_copy(side, at).wait_send()


def over_blend(front_part, back_part):
    transmit = front_part[3:4]
    return jnp.concatenate([front_part[:3] + transmit * back_part[:3], transmit * back_part[3:4]], 0)


def blend_group(received):
    blended = received
    while blended.shape[2] > 1:
        channels, items, sources, owned = blended.shape
        paired = blended.reshape(channels, items, sources // 2, 2, owned)
        blended = over_blend(paired[:, :, :, 0, :], paired[:, :, :, 1, :])
    return blended[:, :, 0, :]


def on_device(density, materials, colors, opacity):
    depth_count, group = lax.axis_size("depth"), lax.axis_size("outer")
    count = depth_count * group
    depth_own, rows, cols = density.shape
    owned = rows * cols // count
    direct = owned % (2 * LANES) == 0 and cols % owned == 0
    width = owned if direct else cols
    size = CHANNELS * width // LANES if direct else 8
    planes = depth_own + 2 * HALO
    out_shape = (3, owned) if direct else (CHANNELS, rows, cols)
    chunks = cols // width
    volume = pltpu.VMEM((planes, rows, cols), jnp.float32)
    tiles = cols // (BLOCK * LANES)
    layers = pl.pallas_call(
        functools.partial(render_kernel, dict(count=count, group=group, direct=direct, width=width)),
        out_shape=jax.ShapeDtypeStruct(out_shape, jnp.float32),
        in_specs=[
            pl.BlockSpec(memory_space=pl.ANY),
            pl.BlockSpec(memory_space=pl.ANY),
            pl.BlockSpec(memory_space=pltpu.SMEM),
            pl.BlockSpec(memory_space=pltpu.SMEM),
        ],
        out_specs=pl.BlockSpec(memory_space=pltpu.VMEM),
        scratch_shapes=[
            volume,
            volume,
            volume,
            pltpu.VMEM(materials.shape, jnp.int32),
            pltpu.VMEM((2 * LANES, BLOCK * LANES), jnp.bfloat16),
            pltpu.VMEM((tiles, CHANNELS * depth_own * rows, 2 * LANES), jnp.bfloat16),
            pltpu.VMEM((CHANNELS * depth_own * rows, cols), jnp.float32),
            pltpu.VMEM((count * size, LANES), jnp.float32),
            pltpu.VMEM((count * size, LANES), jnp.float32),
            pltpu.SemaphoreType.DMA,
            pltpu.SemaphoreType.DMA,
            pltpu.SemaphoreType.DMA((2, chunks)),
            pltpu.SemaphoreType.DMA((2, chunks)),
            pltpu.SemaphoreType.DMA,
            pltpu.SemaphoreType.DMA,
        ],
        compiler_params=pltpu.CompilerParams(
            collective_id=0, has_side_effects=True, vmem_limit_bytes=60 * 1024 * 1024
        ),
    )(density, materials, colors, opacity)
    if direct:
        return layers
    layers = layers.reshape(CHANNELS, depth_count, group, owned)
    merged = blend_group(lax.all_to_all(layers, "outer", split_axis=2, concat_axis=2, tiled=True))
    stacked = merged.reshape(CHANNELS, 1, depth_count, owned)
    layers = blend_group(lax.all_to_all(stacked, "depth", split_axis=2, concat_axis=2, tiled=True))
    return 1.0 - jnp.exp(-4.0 * layers.reshape(CHANNELS, owned)[:3])


def solution(mesh):
    placed = (P(("depth", "outer"), None, None), P(("depth", "outer"), None, None), P(), P())
    return jax.shard_map(
        on_device,
        mesh=mesh,
        in_specs=placed,
        out_specs=P(None, ("depth", "outer")),
        check_vma=False,
    )
```

```python
import functools

import jax
import jax.numpy as jnp
from jax import lax
from jax.experimental import pallas as pl
from jax.experimental.pallas import tpu as pltpu
from jax.sharding import PartitionSpec as P

LIGHT_DIR = (0.64, 0.48, 0.6)
MESH = pl.DeviceIdType.MESH
LANES = 128
HALO = 4
BLOCK = 4
CHANNELS = 4


def shifted(values, amount, axis, at_low, at_high):
    length = values.shape[axis]
    moved = pltpu.roll(values, (-amount) % length, axis)
    index = lax.broadcasted_iota(jnp.int32, values.shape, axis)
    if amount < 0 and at_low:
        moved = jnp.where(index < -amount, 0.0, moved)
    if amount > 0 and at_high:
        moved = jnp.where(index >= length - amount, 0.0, moved)
    return moved


def render_kernel(
    plan, density, materials, colors_in, opacity_in, out, colors, opacity, ext, first, second, labels, spread, coarse, table,
    pieces, inbox, own_sem, label_sem, color_sem, opacity_sem, halo_send, halo_recv, piece_send, piece_recv,
):
    count, group, direct = plan["count"], plan["group"], plan["direct"]
    depth_own, rows, cols = density.shape
    depth_at, outer_at = lax.axis_index("depth"), lax.axis_index("outer")
    me = depth_at * group + outer_at
    planes = depth_own + 2 * HALO

    def device(position):
        return (lax.div(position, group), lax.rem(position, group))

    own_copy = pltpu.make_async_copy(density, ext.at[pl.ds(HALO, depth_own)], own_sem)
    own_copy.start()
    label_copy = pltpu.make_async_copy(materials, labels, label_sem)
    label_copy.start()
    color_copy = pltpu.make_async_copy(colors_in, colors, color_sem)
    color_copy.start()
    opacity_copy = pltpu.make_async_copy(opacity_in, opacity, opacity_sem)
    opacity_copy.start()

    barrier = pltpu.get_barrier_semaphore()
    if direct:
        @pl.loop(1, count)
        def _(step):
            pl.semaphore_signal(barrier, inc=1, device_id=device(lax.rem(me + step, count)), device_id_type=MESH)
        pl.semaphore_wait(barrier, count - 1)
    else:
        for away, there in ((-1, me > 0), (1, me < count - 1)):
            @pl.when(there)
            def _(away=away):
                pl.semaphore_signal(barrier, inc=1, device_id=device(me + away), device_id_type=MESH)
        for there in (me > 0, me < count - 1):
            @pl.when(there)
            def _():
                pl.semaphore_wait(barrier, 1)

    width = plan["width"]
    chunks = cols // width
    ends = [min((at + 1) * width + LANES, cols) for at in range(chunks)]
    begins = [0] + ends[:-1]

    def halo_copy(side, at):
        lanes = pl.ds(begins[at], ends[at] - begins[at])
        if side == 0:
            source, target, to = depth_own - HALO, 0, lax.rem(me + 1, count)
        else:
            source, target, to = 0, depth_own + HALO, lax.rem(me + count - 1, count)
        return pltpu.make_async_remote_copy(
            src_ref=density.at[pl.ds(source, HALO), :, lanes],
            dst_ref=ext.at[pl.ds(target, HALO), :, lanes],
            send_sem=halo_send.at[side, at],
            recv_sem=halo_recv.at[side, at],
            device_id=device(to),
            device_id_type=MESH,
        )

    sends = ((0, me < count - 1), (1, me > 0))
    receives = ((0, me > 0), (1, me < count - 1))

    def start_halo(at):
        for side, there in sends:
            @pl.when(there)
            def _(side=side):
                halo_copy(side, at).start()

    def finish_halo(at):
        for side, there in sends:
            @pl.when(there)
            def _(side=side):
                halo_copy(side, at).wait_send()

    used = [at for at in range(chunks) if begins[at] < ends[at]]
    start_halo(used[0])

    @pl.when(me == 0)
    def _():
        ext[pl.ds(0, HALO)] = jnp.zeros((HALO, rows, cols), jnp.float32)

    @pl.when(me == count - 1)
    def _():
        ext[pl.ds(depth_own + HALO, HALO)] = jnp.zeros((HALO, rows, cols), jnp.float32)

    fine = BLOCK * LANES
    row_at = lax.rem(lax.broadcasted_iota(jnp.int32, (2 * LANES, fine), 0), LANES)
    col_at = lax.div(lax.broadcasted_iota(jnp.int32, (2 * LANES, fine), 1), BLOCK)
    spread[...] = jnp.where(row_at == col_at, 1.0, 0.0).astype(jnp.bfloat16)
    label_copy.wait()
    color_copy.wait()
    opacity_copy.wait()
    tiles = cols // fine

    @pl.loop(0, depth_own, unroll=2)
    def _(plane):
        index = labels[plane]
        index = jnp.concatenate(
            [jnp.broadcast_to(index[row : row + 1], (BLOCK, index.shape[1])) for row in range(rows // BLOCK)], 0
        )
        found = [jnp.zeros(index.shape, jnp.float32) for channel in range(CHANNELS)]
        for material in range(colors.shape[1]):
            chosen = index == material
            for channel in range(CHANNELS - 1):
                found[channel] = jnp.where(chosen, colors[channel, material], found[channel])
            found[-1] = jnp.where(chosen, 0.5 * opacity[material], found[-1])
        for channel in range(CHANNELS):
            high = found[channel].astype(jnp.bfloat16)
            low = (found[channel] - high.astype(jnp.float32)).astype(jnp.bfloat16)
            start = pl.multiple_of((plane * CHANNELS + channel) * rows, rows)
            for tile in range(tiles):
                lanes = slice(tile * LANES, (tile + 1) * LANES)
                coarse[tile, pl.ds(start, rows), :LANES] = high[:, lanes]
                coarse[tile, pl.ds(start, rows), LANES:] = low[:, lanes]

    for tile in range(tiles):
        table[:, tile * fine : (tile + 1) * fine] = jnp.dot(
            coarse[tile], spread[...], preferred_element_type=jnp.float32
        )

    def smooth(source, target, start, stop, low, high):
        lanes = pl.ds(low, high - low)

        @pl.loop(start, stop, unroll=True)
        def _(plane):
            where = me * depth_own - HALO + plane
            inside = jnp.where((where >= 0) & (where < count * depth_own), 1.0, 0.0)
            center = source[plane, :, lanes]
            beside = source[plane - 1, :, lanes] + source[plane + 1, :, lanes]
            beside += shifted(center, -1, 0, True, True) + shifted(center, 1, 0, True, True)
            beside += shifted(center, -1, 1, low == 0, high == cols) + shifted(center, 1, 1, low == 0, high == cols)
            target[plane, :, lanes] = (0.25 * inside) * center + (0.125 * inside) * beside

    own_copy.wait()
    smooth(ext, first, HALO + 1, planes - HALO - 1, 0, cols)
    smooth(first, second, HALO + 2, planes - HALO - 2, 0, cols)

    def differences(minus, plus, minus_two, plus_two):
        return ((plus - minus) + 2.0 * (plus_two - minus_two)) * 0.1

    block = min(width, 2 * LANES)
    for at in range(chunks):
        if at in used:
            if at != used[-1]:
                finish_halo(at)
                start_halo(used[used.index(at) + 1])
            for side, there in receives:
                @pl.when(there)
                def _(side=side, at=at):
                    halo_copy(side, at).wait_recv()
        low, high = max(at * width - LANES, 0), ends[at]
        smooth(ext, first, 1, HALO + 1, low, high)
        smooth(ext, first, planes - HALO - 1, planes - 1, low, high)
        smooth(first, second, 2, HALO + 2, low, high)
        smooth(first, second, planes - HALO - 2, planes - 2, low, high)
        for base in range(at * width, (at + 1) * width, block):
            left, right = max(base - LANES, 0), min(base + block + LANES, cols)

            def shade(plane, carry, base=base, left=left, right=right):
                light, transmit = carry[:3], carry[3]
                own = pl.ds(base, block)
                slot = plane + HALO
                center = second[slot, :, own]
                along = functools.partial(shifted, center, axis=0, at_low=True, at_high=True)
                wide = second[slot, :, pl.ds(left, right - left)]

                def across(amount):
                    moved = shifted(wide, amount, 1, left == 0, right == cols)
                    return moved[:, base - left : base - left + block]

                grad_depth = differences(*(second[slot + step, :, own] for step in (-1, 1, -2, 2)))
                grad_rows = differences(*(along(step) for step in (-1, 1, -2, 2)))
                grad_cols = differences(*(across(step) for step in (-1, 1, -2, 2)))
                facing = LIGHT_DIR[0] * grad_depth + LIGHT_DIR[1] * grad_rows + LIGHT_DIR[2] * grad_cols
                length_sq = grad_depth * grad_depth + grad_rows * grad_rows + grad_cols * grad_cols + 1.0
                shading = 0.1 + 0.9 * jnp.abs(facing) * lax.rsqrt(length_sq)

                def looked_up(channel):
                    start = pl.multiple_of((plane * CHANNELS + channel) * rows, rows)
                    return table[pl.ds(start, rows), own]

                stopped = transmit * (looked_up(3) * (1.0 + jnp.tanh(center)))
                shaded = stopped * shading
                light = tuple(light[channel] + looked_up(channel) * shaded for channel in range(3))
                return light + (transmit - stopped,)

            empty = jnp.zeros((rows, block), jnp.float32)
            layers = lax.fori_loop(0, depth_own, shade, (empty, empty, empty, empty + 1.0), unroll=True)
            for channel in range(CHANNELS):
                if not direct:
                    out[channel, :, pl.ds(base, block)] = layers[channel]
                    continue
                strips = width // LANES
                for strip in range(block // LANES):
                    slot = (base - at * width) // LANES + strip
                    start = at * CHANNELS * strips + channel * strips + slot
                    pieces[pl.ds(start, rows, stride=chunks * CHANNELS * strips), :] = layers[channel][
                        :, strip * LANES : (strip + 1) * LANES
                    ]
        if direct:
            size = CHANNELS * width // LANES

            @pl.loop(0, rows)
            def _(row, at=at):
                to = lax.rem(lax.div(me, chunks) + row, rows) * chunks + at
                here = pl.ds(pl.multiple_of(to * size, size), size)
                there = pl.ds(pl.multiple_of(me * size, size), size)

                @pl.when(to != me)
                def _():
                    pltpu.make_async_remote_copy(
                        src_ref=pieces.at[here],
                        dst_ref=inbox.at[there],
                        send_sem=piece_send,
                        recv_sem=piece_recv,
                        device_id=device(to),
                        device_id_type=MESH,
                    ).start()

                @pl.when(to == me)
                def _():
                    inbox[there, :] = pieces[here, :]

    if direct:
        size = CHANNELS * width // LANES
        strips = width // LANES
        others = pl.ds(0, (count - 1) * size)
        everything = pltpu.make_async_remote_copy(
            src_ref=pieces.at[others],
            dst_ref=inbox.at[others],
            send_sem=piece_send,
            recv_sem=piece_recv,
            device_id=device(lax.rem(me + 1, count)),
            device_id_type=MESH,
        )
        everything.wait_recv()
        total = [jnp.zeros((strips, LANES), jnp.float32) for channel in range(3)]
        left_over = jnp.ones((strips, LANES), jnp.float32)
        for source in range(count):
            base = source * size
            for channel in range(3):
                total[channel] += left_over * inbox[base + channel * strips : base + (channel + 1) * strips, :]
            left_over = left_over * inbox[base + 3 * strips : base + 4 * strips, :]
        for channel in range(3):
            toned = 1.0 - jnp.exp(-4.0 * total[channel])
            for strip in range(strips):
                out[channel : channel + 1, strip * LANES : (strip + 1) * LANES] = toned[strip : strip + 1]
        everything.wait_send()
    finish_halo(used[-1])


def over_blend(front_part, back_part):
    transmit = front_part[3:4]
    return jnp.concatenate([front_part[:3] + transmit * back_part[:3], transmit * back_part[3:4]], 0)


def blend_group(received):
    blended = received
    while blended.shape[2] > 1:
        channels, items, sources, owned = blended.shape
        paired = blended.reshape(channels, items, sources // 2, 2, owned)
        blended = over_blend(paired[:, :, :, 0, :], paired[:, :, :, 1, :])
    return blended[:, :, 0, :]


def on_device(density, materials, colors, opacity):
    depth_count, group = lax.axis_size("depth"), lax.axis_size("outer")
    count = depth_count * group
    depth_own, rows, cols = density.shape
    owned = rows * cols // count
    direct = owned % (2 * LANES) == 0 and cols % owned == 0
    width = owned if direct else cols
    size = CHANNELS * width // LANES if direct else 8
    planes = depth_own + 2 * HALO
    out_shape = (3, owned) if direct else (CHANNELS, rows, cols)
    chunks = cols // width
    volume = pltpu.VMEM((planes, rows, cols), jnp.float32)
    tiles = cols // (BLOCK * LANES)
    layers = pl.pallas_call(
        functools.partial(render_kernel, dict(count=count, group=group, direct=direct, width=width)),
        out_shape=jax.ShapeDtypeStruct(out_shape, jnp.float32),
        in_specs=[
            pl.BlockSpec(memory_space=pl.ANY),
            pl.BlockSpec(memory_space=pl.ANY),
            pl.BlockSpec(memory_space=pl.ANY),
            pl.BlockSpec(memory_space=pl.ANY),
        ],
        out_specs=pl.BlockSpec(memory_space=pltpu.VMEM),
        scratch_shapes=[
            pltpu.SMEM(colors.shape, jnp.float32),
            pltpu.SMEM(opacity.shape, jnp.float32),
            volume,
            volume,
            volume,
            pltpu.VMEM(materials.shape, jnp.int32),
            pltpu.VMEM((2 * LANES, BLOCK * LANES), jnp.bfloat16),
            pltpu.VMEM((tiles, CHANNELS * depth_own * rows, 2 * LANES), jnp.bfloat16),
            pltpu.VMEM((CHANNELS * depth_own * rows, cols), jnp.float32),
            pltpu.VMEM((count * size, LANES), jnp.float32),
            pltpu.VMEM((count * size, LANES), jnp.float32),
            pltpu.SemaphoreType.DMA,
            pltpu.SemaphoreType.DMA,
            pltpu.SemaphoreType.DMA,
            pltpu.SemaphoreType.DMA,
            pltpu.SemaphoreType.DMA((2, chunks)),
            pltpu.SemaphoreType.DMA((2, chunks)),
            pltpu.SemaphoreType.DMA,
            pltpu.SemaphoreType.DMA,
        ],
        compiler_params=pltpu.CompilerParams(
            collective_id=0, has_side_effects=True, vmem_limit_bytes=60 * 1024 * 1024
        ),
    )(density, materials, colors, opacity)
    if direct:
        return layers
    layers = layers.reshape(CHANNELS, depth_count, group, owned)
    merged = blend_group(lax.all_to_all(layers, "outer", split_axis=2, concat_axis=2, tiled=True))
    stacked = merged.reshape(CHANNELS, 1, depth_count, owned)
    layers = blend_group(lax.all_to_all(stacked, "depth", split_axis=2, concat_axis=2, tiled=True))
    return 1.0 - jnp.exp(-4.0 * layers.reshape(CHANNELS, owned)[:3])


def solution(mesh):
    placed = (P(("depth", "outer"), None, None), P(("depth", "outer"), None, None), P(), P())
    return jax.shard_map(
        on_device,
        mesh=mesh,
        in_specs=placed,
        out_specs=P(None, ("depth", "outer")),
        check_vma=False,
    )
```

```python
import functools

import jax
import jax.numpy as jnp
from jax import lax
from jax.experimental import pallas as pl
from jax.experimental.pallas import tpu as pltpu
from jax.sharding import PartitionSpec as P

LIGHT_DIR = (0.64, 0.48, 0.6)
MESH = pl.DeviceIdType.MESH
LANES = 128
HALO = 4
BLOCK = 4
CHANNELS = 4


def shifted(values, amount, axis, at_low, at_high):
    length = values.shape[axis]
    moved = pltpu.roll(values, (-amount) % length, axis)
    index = lax.broadcasted_iota(jnp.int32, values.shape, axis)
    if amount < 0 and at_low:
        moved = jnp.where(index < -amount, 0.0, moved)
    if amount > 0 and at_high:
        moved = jnp.where(index >= length - amount, 0.0, moved)
    return moved


def render_kernel(
    plan, density, materials, colors_in, opacity_in, out, colors, opacity, ext, first, second, labels, spread, coarse, table,
    pieces, inbox, own_sem, label_sem, color_sem, opacity_sem, halo_send, halo_recv, piece_send, piece_recv,
):
    count, group, direct = plan["count"], plan["group"], plan["direct"]
    depth_own, rows, cols = density.shape
    depth_at, outer_at = lax.axis_index("depth"), lax.axis_index("outer")
    me = depth_at * group + outer_at
    planes = depth_own + 2 * HALO

    def device(position):
        return (lax.div(position, group), lax.rem(position, group))

    own_copy = pltpu.make_async_copy(density, ext.at[pl.ds(HALO, depth_own)], own_sem)
    own_copy.start()
    label_copy = pltpu.make_async_copy(materials, labels, label_sem)
    label_copy.start()
    color_copy = pltpu.make_async_copy(colors_in, colors, color_sem)
    color_copy.start()
    opacity_copy = pltpu.make_async_copy(opacity_in, opacity, opacity_sem)
    opacity_copy.start()

    barrier = pltpu.get_barrier_semaphore()
    if direct:
        @pl.loop(1, count)
        def _(step):
            pl.semaphore_signal(barrier, inc=1, device_id=device(lax.rem(me + step, count)), device_id_type=MESH)
        pl.semaphore_wait(barrier, count - 1)
    else:
        for away, there in ((-1, me > 0), (1, me < count - 1)):
            @pl.when(there)
            def _(away=away):
                pl.semaphore_signal(barrier, inc=1, device_id=device(me + away), device_id_type=MESH)
        for there in (me > 0, me < count - 1):
            @pl.when(there)
            def _():
                pl.semaphore_wait(barrier, 1)

    width, parts = plan["width"], plan["parts"]
    chunks = cols // width
    ends = [min((at + 1) * width + LANES, cols) for at in range(chunks)]
    begins = [0] + ends[:-1]

    def halo_copy(side, at):
        lanes = pl.ds(begins[at], ends[at] - begins[at])
        if side == 0:
            source, target, to = depth_own - HALO, 0, lax.rem(me + 1, count)
        else:
            source, target, to = 0, depth_own + HALO, lax.rem(me + count - 1, count)
        return pltpu.make_async_remote_copy(
            src_ref=density.at[pl.ds(source, HALO), :, lanes],
            dst_ref=ext.at[pl.ds(target, HALO), :, lanes],
            send_sem=halo_send.at[side, at],
            recv_sem=halo_recv.at[side, at],
            device_id=device(to),
            device_id_type=MESH,
        )

    sends = ((0, me < count - 1), (1, me > 0))
    receives = ((0, me > 0), (1, me < count - 1))

    def start_halo(at):
        for side, there in sends:
            @pl.when(there)
            def _(side=side):
                halo_copy(side, at).start()

    def finish_halo(at):
        for side, there in sends:
            @pl.when(there)
            def _(side=side):
                halo_copy(side, at).wait_send()

    used = [at for at in range(chunks) if begins[at] < ends[at]]
    for at in used[:2]:
        start_halo(at)

    @pl.when(me == 0)
    def _():
        ext[pl.ds(0, HALO)] = jnp.zeros((HALO, rows, cols), jnp.float32)

    @pl.when(me == count - 1)
    def _():
        ext[pl.ds(depth_own + HALO, HALO)] = jnp.zeros((HALO, rows, cols), jnp.float32)

    fine = BLOCK * LANES
    row_at = lax.rem(lax.broadcasted_iota(jnp.int32, (2 * LANES, fine), 0), LANES)
    col_at = lax.div(lax.broadcasted_iota(jnp.int32, (2 * LANES, fine), 1), BLOCK)
    spread[...] = jnp.where(row_at == col_at, 1.0, 0.0).astype(jnp.bfloat16)
    label_copy.wait()
    color_copy.wait()
    opacity_copy.wait()
    tiles = cols // fine

    @pl.loop(0, depth_own, unroll=2)
    def _(plane):
        index = labels[plane]
        index = jnp.concatenate(
            [jnp.broadcast_to(index[row : row + 1], (BLOCK, index.shape[1])) for row in range(rows // BLOCK)], 0
        )
        found = [jnp.zeros(index.shape, jnp.float32) for channel in range(CHANNELS)]
        for material in range(colors.shape[1]):
            chosen = index == material
            for channel in range(CHANNELS - 1):
                found[channel] = jnp.where(chosen, colors[channel, material], found[channel])
            found[-1] = jnp.where(chosen, 0.5 * opacity[material], found[-1])
        for channel in range(CHANNELS):
            high = found[channel].astype(jnp.bfloat16)
            low = (found[channel] - high.astype(jnp.float32)).astype(jnp.bfloat16)
            start = pl.multiple_of((plane * CHANNELS + channel) * rows, rows)
            for tile in range(tiles):
                lanes = slice(tile * LANES, (tile + 1) * LANES)
                coarse[tile, pl.ds(start, rows), :LANES] = high[:, lanes]
                coarse[tile, pl.ds(start, rows), LANES:] = low[:, lanes]

    for tile in range(tiles):
        table[:, tile * fine : (tile + 1) * fine] = jnp.dot(
            coarse[tile], spread[...], preferred_element_type=jnp.float32
        )

    def smooth(source, target, start, stop, low, high, keep=0):
        lanes = pl.ds(low, high - low)

        @pl.loop(start, stop, unroll=True)
        def _(plane):
            where = me * depth_own - HALO + plane
            inside = jnp.where((where >= 0) & (where < count * depth_own), 1.0, 0.0)
            center = source[plane, :, lanes]
            beside = source[plane - 1, :, lanes] + source[plane + 1, :, lanes]
            beside += shifted(center, -1, 0, True, True) + shifted(center, 1, 0, True, True)
            beside += shifted(center, -1, 1, low == 0, high == cols) + shifted(center, 1, 1, low == 0, high == cols)
            smoothed = (0.25 * inside) * center + (0.125 * inside) * beside
            target[plane, :, pl.ds(low + keep, high - low - keep)] = smoothed[:, keep:]

    own_copy.wait()
    smooth(ext, first, HALO + 1, planes - HALO - 1, 0, cols)
    smooth(first, second, HALO + 2, planes - HALO - 2, 0, cols)

    def differences(minus, plus, minus_two, plus_two):
        return ((plus - minus) + 2.0 * (plus_two - minus_two)) * 0.1

    block = min(width, 2 * LANES)
    for at in range(chunks):
        if at in used:
            if used.index(at) + 2 < len(used):
                finish_halo(at)
                start_halo(used[used.index(at) + 2])
            for side, there in receives:
                @pl.when(there)
                def _(side=side, at=at):
                    halo_copy(side, at).wait_recv()
        low, high = max(at * width - LANES, 0), ends[at]
        keep = at * width - low
        smooth(ext, first, 1, HALO + 1, low, high, keep)
        smooth(ext, first, planes - HALO - 1, planes - 1, low, high, keep)
        smooth(first, second, 2, HALO + 2, low, high, keep)
        smooth(first, second, planes - HALO - 2, planes - 2, low, high, keep)
        for base in range(at * width, (at + 1) * width, block):
            left, right = max(base - LANES, 0), min(base + block + LANES, cols)

            def shade(plane, carry, base=base, left=left, right=right):
                light, transmit = carry[:3], carry[3]
                own = pl.ds(base, block)
                slot = plane + HALO
                center = second[slot, :, own]
                along = functools.partial(shifted, center, axis=0, at_low=True, at_high=True)
                wide = second[slot, :, pl.ds(left, right - left)]

                def across(amount):
                    moved = shifted(wide, amount, 1, left == 0, right == cols)
                    return moved[:, base - left : base - left + block]

                grad_depth = differences(*(second[slot + step, :, own] for step in (-1, 1, -2, 2)))
                grad_rows = differences(*(along(step) for step in (-1, 1, -2, 2)))
                grad_cols = differences(*(across(step) for step in (-1, 1, -2, 2)))
                facing = LIGHT_DIR[0] * grad_depth + LIGHT_DIR[1] * grad_rows + LIGHT_DIR[2] * grad_cols
                length_sq = grad_depth * grad_depth + grad_rows * grad_rows + grad_cols * grad_cols + 1.0
                shading = 0.1 + 0.9 * jnp.abs(facing) * lax.rsqrt(length_sq)

                def looked_up(channel):
                    start = pl.multiple_of((plane * CHANNELS + channel) * rows, rows)
                    return table[pl.ds(start, rows), own]

                stopped = transmit * (looked_up(3) * (1.0 + jnp.tanh(center)))
                shaded = stopped * shading
                light = tuple(light[channel] + looked_up(channel) * shaded for channel in range(3))
                return light + (transmit - stopped,)

            empty = jnp.zeros((rows, block), jnp.float32)
            layers = lax.fori_loop(0, depth_own, shade, (empty, empty, empty, empty + 1.0), unroll=True)
            for channel in range(CHANNELS):
                if not direct:
                    out[channel, :, pl.ds(base, block)] = layers[channel]
                    continue
                strips = width // LANES
                for strip in range(block // LANES):
                    slot = (base - at * width) // LANES + strip
                    start = at * CHANNELS * strips + channel * strips + slot
                    pieces[pl.ds(start, rows, stride=chunks * CHANNELS * strips), :] = layers[channel][
                        :, strip * LANES : (strip + 1) * LANES
                    ]
        if direct:
            size = CHANNELS * width // LANES

            @pl.loop(0, rows)
            def _(row, at=at):
                to_row = lax.rem(lax.div(me, chunks // parts) + row, rows)
                to = to_row * (chunks // parts) + at // parts
                here = pl.ds(pl.multiple_of((to_row * chunks + at) * size, size), size)
                there = pl.ds(pl.multiple_of((me * parts + at % parts) * size, size), size)

                @pl.when(to != me)
                def _():
                    pltpu.make_async_remote_copy(
                        src_ref=pieces.at[here],
                        dst_ref=inbox.at[there],
                        send_sem=piece_send,
                        recv_sem=piece_recv,
                        device_id=device(to),
                        device_id_type=MESH,
                    ).start()

                @pl.when(to == me)
                def _():
                    inbox[there, :] = pieces[here, :]

    if direct:
        size = CHANNELS * width // LANES
        strips = width // LANES
        others = pl.ds(0, (count - 1) * parts * size)
        everything = pltpu.make_async_remote_copy(
            src_ref=pieces.at[others],
            dst_ref=inbox.at[others],
            send_sem=piece_send,
            recv_sem=piece_recv,
            device_id=device(lax.rem(me + 1, count)),
            device_id_type=MESH,
        )
        everything.wait_recv()
        for part in range(parts):
            total = [jnp.zeros((strips, LANES), jnp.float32) for channel in range(3)]
            left_over = jnp.ones((strips, LANES), jnp.float32)
            for source in range(count):
                base = (source * parts + part) * size
                for channel in range(3):
                    total[channel] += left_over * inbox[base + channel * strips : base + (channel + 1) * strips, :]
                left_over = left_over * inbox[base + 3 * strips : base + 4 * strips, :]
            for channel in range(3):
                toned = 1.0 - jnp.exp(-4.0 * total[channel])
                for strip in range(strips):
                    lane = part * width + strip * LANES
                    out[channel : channel + 1, lane : lane + LANES] = toned[strip : strip + 1]
        everything.wait_send()
    for at in used[-2:]:
        finish_halo(at)


def over_blend(front_part, back_part):
    transmit = front_part[3:4]
    return jnp.concatenate([front_part[:3] + transmit * back_part[:3], transmit * back_part[3:4]], 0)


def blend_group(received):
    blended = received
    while blended.shape[2] > 1:
        channels, items, sources, owned = blended.shape
        paired = blended.reshape(channels, items, sources // 2, 2, owned)
        blended = over_blend(paired[:, :, :, 0, :], paired[:, :, :, 1, :])
    return blended[:, :, 0, :]


def on_device(density, materials, colors, opacity):
    depth_count, group = lax.axis_size("depth"), lax.axis_size("outer")
    count = depth_count * group
    depth_own, rows, cols = density.shape
    owned = rows * cols // count
    direct = owned % (2 * LANES) == 0 and cols % owned == 0
    width = 2 * LANES if direct else cols
    parts = owned // width if direct else 1
    size = CHANNELS * width // LANES if direct else 8
    planes = depth_own + 2 * HALO
    out_shape = (3, owned) if direct else (CHANNELS, rows, cols)
    chunks = cols // width
    volume = pltpu.VMEM((planes, rows, cols), jnp.float32)
    tiles = cols // (BLOCK * LANES)
    layers = pl.pallas_call(
        functools.partial(render_kernel, dict(count=count, group=group, direct=direct, width=width, parts=parts)),
        out_shape=jax.ShapeDtypeStruct(out_shape, jnp.float32),
        in_specs=[
            pl.BlockSpec(memory_space=pl.ANY),
            pl.BlockSpec(memory_space=pl.ANY),
            pl.BlockSpec(memory_space=pl.ANY),
            pl.BlockSpec(memory_space=pl.ANY),
        ],
        out_specs=pl.BlockSpec(memory_space=pltpu.VMEM),
        scratch_shapes=[
            pltpu.SMEM(colors.shape, jnp.float32),
            pltpu.SMEM(opacity.shape, jnp.float32),
            volume,
            volume,
            volume,
            pltpu.VMEM(materials.shape, jnp.int32),
            pltpu.VMEM((2 * LANES, BLOCK * LANES), jnp.bfloat16),
            pltpu.VMEM((tiles, CHANNELS * depth_own * rows, 2 * LANES), jnp.bfloat16),
            pltpu.VMEM((CHANNELS * depth_own * rows, cols), jnp.float32),
            pltpu.VMEM((count * parts * size, LANES), jnp.float32),
            pltpu.VMEM((count * parts * size, LANES), jnp.float32),
            pltpu.SemaphoreType.DMA,
            pltpu.SemaphoreType.DMA,
            pltpu.SemaphoreType.DMA,
            pltpu.SemaphoreType.DMA,
            pltpu.SemaphoreType.DMA((2, chunks)),
            pltpu.SemaphoreType.DMA((2, chunks)),
            pltpu.SemaphoreType.DMA,
            pltpu.SemaphoreType.DMA,
        ],
        compiler_params=pltpu.CompilerParams(
            collective_id=0, has_side_effects=True, vmem_limit_bytes=60 * 1024 * 1024
        ),
    )(density, materials, colors, opacity)
    if direct:
        return layers
    layers = layers.reshape(CHANNELS, depth_count, group, owned)
    merged = blend_group(lax.all_to_all(layers, "outer", split_axis=2, concat_axis=2, tiled=True))
    stacked = merged.reshape(CHANNELS, 1, depth_count, owned)
    layers = blend_group(lax.all_to_all(stacked, "depth", split_axis=2, concat_axis=2, tiled=True))
    return 1.0 - jnp.exp(-4.0 * layers.reshape(CHANNELS, owned)[:3])


def solution(mesh):
    placed = (P(("depth", "outer"), None, None), P(("depth", "outer"), None, None), P(), P())
    return jax.shard_map(
        on_device,
        mesh=mesh,
        in_specs=placed,
        out_specs=P(None, ("depth", "outer")),
        check_vma=False,
    )
```

```python
import functools

import jax
import jax.numpy as jnp
from jax import lax
from jax.experimental import pallas as pl
from jax.experimental.pallas import tpu as pltpu
from jax.sharding import PartitionSpec as P

LIGHT_DIR = (0.64, 0.48, 0.6)
MESH = pl.DeviceIdType.MESH
LANES = 128
HALO = 4
BLOCK = 4
CHANNELS = 4


def shifted(values, amount, axis, at_low, at_high):
    length = values.shape[axis]
    moved = pltpu.roll(values, (-amount) % length, axis)
    index = lax.broadcasted_iota(jnp.int32, values.shape, axis)
    if amount < 0 and at_low:
        moved = jnp.where(index < -amount, 0.0, moved)
    if amount > 0 and at_high:
        moved = jnp.where(index >= length - amount, 0.0, moved)
    return moved


def render_kernel(
    plan, density, materials, colors_in, opacity_in, out, colors, opacity, ext, first, second, labels, spread, coarse, table,
    pieces, inbox, own_sem, label_sem, color_sem, opacity_sem, halo_send, halo_recv, piece_send, piece_recv,
):
    count, group, direct = plan["count"], plan["group"], plan["direct"]
    depth_own, rows, cols = density.shape
    depth_at, outer_at = lax.axis_index("depth"), lax.axis_index("outer")
    me = depth_at * group + outer_at
    planes = depth_own + 2 * HALO

    def device(position):
        return (lax.div(position, group), lax.rem(position, group))

    own_copy = pltpu.make_async_copy(density, ext.at[pl.ds(HALO, depth_own)], own_sem)
    own_copy.start()
    label_copy = pltpu.make_async_copy(materials, labels, label_sem)
    label_copy.start()
    color_copy = pltpu.make_async_copy(colors_in, colors, color_sem)
    color_copy.start()
    opacity_copy = pltpu.make_async_copy(opacity_in, opacity, opacity_sem)
    opacity_copy.start()

    barrier = pltpu.get_barrier_semaphore()
    if direct:
        @pl.loop(1, count, unroll=True)
        def _(step):
            pl.semaphore_signal(barrier, inc=1, device_id=device(lax.rem(me + step, count)), device_id_type=MESH)
        pl.semaphore_wait(barrier, count - 1)
    else:
        for away, there in ((-1, me > 0), (1, me < count - 1)):
            @pl.when(there)
            def _(away=away):
                pl.semaphore_signal(barrier, inc=1, device_id=device(me + away), device_id_type=MESH)
        for there in (me > 0, me < count - 1):
            @pl.when(there)
            def _():
                pl.semaphore_wait(barrier, 1)

    width = plan["width"]
    chunks = cols // width
    ends = [min((at + 1) * width + LANES, cols) for at in range(chunks)]
    begins = [0] + ends[:-1]

    def halo_copy(side, at):
        lanes = pl.ds(begins[at], ends[at] - begins[at])
        if side == 0:
            source, target, to = depth_own - HALO, 0, lax.rem(me + 1, count)
        else:
            source, target, to = 0, depth_own + HALO, lax.rem(me + count - 1, count)
        return pltpu.make_async_remote_copy(
            src_ref=density.at[pl.ds(source, HALO), :, lanes],
            dst_ref=ext.at[pl.ds(target, HALO), :, lanes],
            send_sem=halo_send.at[side, at],
            recv_sem=halo_recv.at[side, at],
            device_id=device(to),
            device_id_type=MESH,
        )

    sends = ((0, me < count - 1), (1, me > 0))
    receives = ((0, me > 0), (1, me < count - 1))

    def start_halo(at):
        for side, there in sends:
            @pl.when(there)
            def _(side=side):
                halo_copy(side, at).start()

    def finish_halo(at):
        for side, there in sends:
            @pl.when(there)
            def _(side=side):
                halo_copy(side, at).wait_send()

    used = [at for at in range(chunks) if begins[at] < ends[at]]
    for at in used:
        start_halo(at)

    @pl.when(me == 0)
    def _():
        ext[pl.ds(0, HALO)] = jnp.zeros((HALO, rows, cols), jnp.float32)

    @pl.when(me == count - 1)
    def _():
        ext[pl.ds(depth_own + HALO, HALO)] = jnp.zeros((HALO, rows, cols), jnp.float32)

    fine = BLOCK * LANES
    row_at = lax.rem(lax.broadcasted_iota(jnp.int32, (2 * LANES, fine), 0), LANES)
    col_at = lax.div(lax.broadcasted_iota(jnp.int32, (2 * LANES, fine), 1), BLOCK)
    spread[...] = jnp.where(row_at == col_at, 1.0, 0.0).astype(jnp.bfloat16)
    label_copy.wait()
    color_copy.wait()
    opacity_copy.wait()
    tiles = cols // fine

    @pl.loop(0, depth_own, unroll=2)
    def _(plane):
        index = labels[plane]
        index = jnp.concatenate(
            [jnp.broadcast_to(index[row : row + 1], (BLOCK, index.shape[1])) for row in range(rows // BLOCK)], 0
        )
        found = [jnp.zeros(index.shape, jnp.float32) for channel in range(CHANNELS)]
        for material in range(colors.shape[1]):
            chosen = index == material
            for channel in range(CHANNELS - 1):
                found[channel] = jnp.where(chosen, colors[channel, material], found[channel])
            found[-1] = jnp.where(chosen, 0.5 * opacity[material], found[-1])
        for channel in range(CHANNELS):
            high = found[channel].astype(jnp.bfloat16)
            low = (found[channel] - high.astype(jnp.float32)).astype(jnp.bfloat16)
            start = pl.multiple_of((plane * CHANNELS + channel) * rows, rows)
            for tile in range(tiles):
                lanes = slice(tile * LANES, (tile + 1) * LANES)
                coarse[tile, pl.ds(start, rows), :LANES] = high[:, lanes]
                coarse[tile, pl.ds(start, rows), LANES:] = low[:, lanes]

    for tile in range(tiles):
        table[:, tile * fine : (tile + 1) * fine] = jnp.dot(
            coarse[tile], spread[...], preferred_element_type=jnp.float32
        )

    def smooth(source, target, start, stop, low, high):
        lanes = pl.ds(low, high - low)

        @pl.loop(start, stop, unroll=True)
        def _(plane):
            where = me * depth_own - HALO + plane
            inside = jnp.where((where >= 0) & (where < count * depth_own), 1.0, 0.0)
            center = source[plane, :, lanes]
            beside = source[plane - 1, :, lanes] + source[plane + 1, :, lanes]
            beside += shifted(center, -1, 0, True, True) + shifted(center, 1, 0, True, True)
            beside += shifted(center, -1, 1, low == 0, high == cols) + shifted(center, 1, 1, low == 0, high == cols)
            target[plane, :, lanes] = (0.25 * inside) * center + (0.125 * inside) * beside

    own_copy.wait()
    smooth(ext, first, HALO + 1, planes - HALO - 1, 0, cols)
    smooth(first, second, HALO + 2, planes - HALO - 2, 0, cols)

    def differences(minus, plus, minus_two, plus_two):
        return ((plus - minus) + 2.0 * (plus_two - minus_two)) * 0.1

    block = min(width, 2 * LANES)
    for at in range(chunks):
        if at in used:
            for side, there in receives:
                @pl.when(there)
                def _(side=side, at=at):
                    halo_copy(side, at).wait_recv()
        low, high = max(at * width - LANES, 0), ends[at]
        smooth(ext, first, 1, HALO + 1, low, high)
        smooth(ext, first, planes - HALO - 1, planes - 1, low, high)
        smooth(first, second, 2, HALO + 2, low, high)
        smooth(first, second, planes - HALO - 2, planes - 2, low, high)
        for base in range(at * width, (at + 1) * width, block):
            left, right = max(base - LANES, 0), min(base + block + LANES, cols)

            def shade(plane, carry, base=base, left=left, right=right):
                light, transmit = carry[:3], carry[3]
                own = pl.ds(base, block)
                slot = plane + HALO
                center = second[slot, :, own]
                along = functools.partial(shifted, center, axis=0, at_low=True, at_high=True)
                wide = second[slot, :, pl.ds(left, right - left)]

                def across(amount):
                    moved = shifted(wide, amount, 1, left == 0, right == cols)
                    return moved[:, base - left : base - left + block]

                grad_depth = differences(*(second[slot + step, :, own] for step in (-1, 1, -2, 2)))
                grad_rows = differences(*(along(step) for step in (-1, 1, -2, 2)))
                grad_cols = differences(*(across(step) for step in (-1, 1, -2, 2)))
                facing = LIGHT_DIR[0] * grad_depth + LIGHT_DIR[1] * grad_rows + LIGHT_DIR[2] * grad_cols
                length_sq = grad_depth * grad_depth + grad_rows * grad_rows + grad_cols * grad_cols + 1.0
                shading = 0.1 + 0.9 * jnp.abs(facing) * lax.rsqrt(length_sq)

                def looked_up(channel):
                    start = pl.multiple_of((plane * CHANNELS + channel) * rows, rows)
                    return table[pl.ds(start, rows), own]

                stopped = transmit * (looked_up(3) * (1.0 + jnp.tanh(center)))
                shaded = stopped * shading
                light = tuple(light[channel] + looked_up(channel) * shaded for channel in range(3))
                return light + (transmit - stopped,)

            empty = jnp.zeros((rows, block), jnp.float32)
            layers = lax.fori_loop(0, depth_own, shade, (empty, empty, empty, empty + 1.0), unroll=True)
            for channel in range(CHANNELS):
                if not direct:
                    out[channel, :, pl.ds(base, block)] = layers[channel]
                    continue
                strips = width // LANES
                for strip in range(block // LANES):
                    slot = (base - at * width) // LANES + strip
                    start = at * CHANNELS * strips + channel * strips + slot
                    pieces[pl.ds(start, rows, stride=chunks * CHANNELS * strips), :] = layers[channel][
                        :, strip * LANES : (strip + 1) * LANES
                    ]
        if direct:
            size = CHANNELS * width // LANES

            @pl.loop(0, rows)
            def _(row, at=at):
                to = lax.rem(lax.div(me, chunks) + row, rows) * chunks + at
                here = pl.ds(pl.multiple_of(to * size, size), size)
                there = pl.ds(pl.multiple_of(me * size, size), size)

                @pl.when(to != me)
                def _():
                    pltpu.make_async_remote_copy(
                        src_ref=pieces.at[here],
                        dst_ref=inbox.at[there],
                        send_sem=piece_send,
                        recv_sem=piece_recv,
                        device_id=device(to),
                        device_id_type=MESH,
                    ).start()

                @pl.when(to == me)
                def _():
                    inbox[there, :] = pieces[here, :]

    if direct:
        size = CHANNELS * width // LANES
        strips = width // LANES
        others = pl.ds(0, (count - 1) * size)
        everything = pltpu.make_async_remote_copy(
            src_ref=pieces.at[others],
            dst_ref=inbox.at[others],
            send_sem=piece_send,
            recv_sem=piece_recv,
            device_id=device(lax.rem(me + 1, count)),
            device_id_type=MESH,
        )
        everything.wait_recv()
        total = [jnp.zeros((strips, LANES), jnp.float32) for channel in range(3)]
        left_over = jnp.ones((strips, LANES), jnp.float32)
        for source in range(count):
            base = source * size
            for channel in range(3):
                total[channel] += left_over * inbox[base + channel * strips : base + (channel + 1) * strips, :]
            left_over = left_over * inbox[base + 3 * strips : base + 4 * strips, :]
        for channel in range(3):
            toned = 1.0 - jnp.exp(-4.0 * total[channel])
            for strip in range(strips):
                out[channel : channel + 1, strip * LANES : (strip + 1) * LANES] = toned[strip : strip + 1]
        everything.wait_send()
    for at in used:
        finish_halo(at)


def over_blend(front_part, back_part):
    transmit = front_part[3:4]
    return jnp.concatenate([front_part[:3] + transmit * back_part[:3], transmit * back_part[3:4]], 0)


def blend_group(received):
    blended = received
    while blended.shape[2] > 1:
        channels, items, sources, owned = blended.shape
        paired = blended.reshape(channels, items, sources // 2, 2, owned)
        blended = over_blend(paired[:, :, :, 0, :], paired[:, :, :, 1, :])
    return blended[:, :, 0, :]


def on_device(density, materials, colors, opacity):
    depth_count, group = lax.axis_size("depth"), lax.axis_size("outer")
    count = depth_count * group
    depth_own, rows, cols = density.shape
    owned = rows * cols // count
    direct = owned % (2 * LANES) == 0 and cols % owned == 0
    width = owned if direct else cols
    size = CHANNELS * width // LANES if direct else 8
    planes = depth_own + 2 * HALO
    out_shape = (3, owned) if direct else (CHANNELS, rows, cols)
    chunks = cols // width
    volume = pltpu.VMEM((planes, rows, cols), jnp.float32)
    tiles = cols // (BLOCK * LANES)
    layers = pl.pallas_call(
        functools.partial(render_kernel, dict(count=count, group=group, direct=direct, width=width)),
        out_shape=jax.ShapeDtypeStruct(out_shape, jnp.float32),
        in_specs=[
            pl.BlockSpec(memory_space=pl.ANY),
            pl.BlockSpec(memory_space=pl.ANY),
            pl.BlockSpec(memory_space=pl.ANY),
            pl.BlockSpec(memory_space=pl.ANY),
        ],
        out_specs=pl.BlockSpec(memory_space=pltpu.VMEM),
        scratch_shapes=[
            pltpu.SMEM(colors.shape, jnp.float32),
            pltpu.SMEM(opacity.shape, jnp.float32),
            volume,
            volume,
            volume,
            pltpu.VMEM(materials.shape, jnp.int32),
            pltpu.VMEM((2 * LANES, BLOCK * LANES), jnp.bfloat16),
            pltpu.VMEM((tiles, CHANNELS * depth_own * rows, 2 * LANES), jnp.bfloat16),
            pltpu.VMEM((CHANNELS * depth_own * rows, cols), jnp.float32),
            pltpu.VMEM((count * size, LANES), jnp.float32),
            pltpu.VMEM((count * size, LANES), jnp.float32),
            pltpu.SemaphoreType.DMA,
            pltpu.SemaphoreType.DMA,
            pltpu.SemaphoreType.DMA,
            pltpu.SemaphoreType.DMA,
            pltpu.SemaphoreType.DMA((2, chunks)),
            pltpu.SemaphoreType.DMA((2, chunks)),
            pltpu.SemaphoreType.DMA,
            pltpu.SemaphoreType.DMA,
        ],
        compiler_params=pltpu.CompilerParams(
            collective_id=0, has_side_effects=True, vmem_limit_bytes=60 * 1024 * 1024
        ),
    )(density, materials, colors, opacity)
    if direct:
        return layers
    layers = layers.reshape(CHANNELS, depth_count, group, owned)
    merged = blend_group(lax.all_to_all(layers, "outer", split_axis=2, concat_axis=2, tiled=True))
    stacked = merged.reshape(CHANNELS, 1, depth_count, owned)
    layers = blend_group(lax.all_to_all(stacked, "depth", split_axis=2, concat_axis=2, tiled=True))
    return 1.0 - jnp.exp(-4.0 * layers.reshape(CHANNELS, owned)[:3])


def solution(mesh):
    placed = (P(("depth", "outer"), None, None), P(("depth", "outer"), None, None), P(), P())
    return jax.shard_map(
        on_device,
        mesh=mesh,
        in_specs=placed,
        out_specs=P(None, ("depth", "outer")),
        check_vma=False,
    )
```
